256 devices in a mesh: grp: 8 (over y, core), rep: 32 (over x, z).
Axes of the slice: x: 4, y: 4, z: 8, core: 2. Of those that a mesh axis runs over, the one named last changes fastest.
Arguments:
- tokens: bfloat16 [8, 2048, 3072], P('grp', 'rep'), may hold values from -13 to 13
- upstream: bfloat16 [8, 2048, 12288], P('grp', None, 'rep'), may hold values from -0.86178639 to 0.86178639
- momentum: bfloat16 [3072, 12288], P(None, 'rep'), may hold values from -6 to 6
- worker_error: bfloat16 [8, 3072, 12288], P('grp', None, 'rep'), may hold values from -4 to 4
- server_error: float32 [3072, 12288], P('grp', 'rep'), may hold values from -4 to 4
Outputs:
- new_momentum: bfloat16 [3072, 12288], P(None, 'rep')
- new_worker_error: bfloat16 [8, 3072, 12288], P('grp', None, 'rep')
- new_server_error: float32 [3072, 12288], P('grp', 'rep')
The draws below stay inside these ranges and needn't reach their ends.
All inputs are finite; a program needn't handle non-finite values.
Results may differ from the reference program's by a relative error of at most 0.011.
Values may be sent and summed in bfloat16 or wider, within the bound.
A program may use at most 128 MiB of HBM per device.

```python
import math
import jax
import jax.numpy as jnp
from jax import lax

D = 3072
FF = 12288
TOK = 2048
WORKERS = 8
N_GRP = 8
N_REP = 32


def column_scales(key, count):
    return jnp.exp(jax.random.uniform(key, (count,), jnp.float32, -1.1513, 1.1513))


def draw_tokens(key, part):
    key = jax.random.fold_in(key, 11)
    noise_key, column_key = jax.random.split(key, 2)
    values = jax.random.truncated_normal(noise_key, -4.0, 4.0, (WORKERS, TOK, D), jnp.float32)
    return (values * column_scales(column_key, D)).astype(jnp.bfloat16)


def draw_upstream(key, part):
    key = jax.random.fold_in(key, 23)
    noise_key, column_key = jax.random.split(key, 2)
    values = jax.random.truncated_normal(noise_key, -4.0, 4.0, (WORKERS, TOK, FF), jnp.float32)
    values = values * column_scales(column_key, FF) * (3.0 / math.sqrt(TOK))
    return values.astype(jnp.bfloat16)


def block_levels(own_key, shape, cuts, low, high):
    level, own = 1.0, jax.random.fold_in(own_key, 6)
    for dim, blocks in cuts:
        steps = jnp.exp(jax.random.uniform(jax.random.fold_in(own, dim), (blocks,), jnp.float32, low / len(cuts), high / len(cuts)))
        level = level * jnp.repeat(steps, shape[dim] // blocks).reshape([-1 if axis == dim else 1 for axis in range(len(shape))])
    return level


def noise(key, extent, width, limit, cuts=(), kind=jnp.bfloat16):
    loudness = block_levels(key, extent, cuts, -0.22, 0.18) if cuts else 1.0
    result = jax.random.normal(key, extent, jnp.float32) * width * loudness
    return jnp.minimum(jnp.maximum(result, -limit), limit).astype(kind)


def setup_inputs(seed: int = 0) -> dict:
    keys = jax.random.split(jax.random.key(seed), 6)
    tokens = draw_tokens(jax.random.fold_in(keys[5], 71), 0)
    upstream = draw_upstream(jax.random.fold_in(keys[5], 71), 0)
    momentum = noise(keys[2], (D, FF), 1.0, 6.0, ((1, 32),))
    worker_error = noise(keys[3], (WORKERS, D, FF), 0.3, 4.0, ((0, 8), (2, 32)))
    server_error = noise(keys[4], (D, FF), 0.3, 4.0, ((0, 8), (1, 32)), jnp.float32)
    return {"tokens": tokens, "upstream": upstream, "momentum": momentum, "worker_error": worker_error, "server_error": server_error}


DECAY_RATE = 0.9
LINEAR_SPAN = 0.0625
EPSILON = 1e-06

def compress(matrix):
    blocks = matrix.reshape(N_GRP, D // N_GRP, N_REP, FF // N_REP)
    energy = lax.optimization_barrier(jnp.mean(blocks * blocks, axis=(1, 3), keepdims=True))
    scales = jnp.sqrt(energy + EPSILON).astype(jnp.bfloat16)
    widened = lax.optimization_barrier(scales).astype(jnp.float32)
    levels = jnp.clip(blocks / (LINEAR_SPAN * widened), -1.0, 1.0).astype(jnp.bfloat16)
    decoded = widened * lax.optimization_barrier(levels).astype(jnp.float32)
    return decoded.reshape(D, FF)

def reference(tokens, upstream, momentum, worker_error, server_error):
    decayed = DECAY_RATE * momentum.astype(jnp.float32)

    def visit(running, bundle):
        inputs, upstream_rows, carried = bundle
        gradient = jnp.dot(inputs.T, upstream_rows, preferred_element_type=jnp.float32)
        buffer = decayed + (1.0 - DECAY_RATE) * gradient + carried.astype(jnp.float32)
        decoded = compress(buffer)
        return (running + decoded, (buffer - decoded).astype(jnp.bfloat16))
    running, new_worker_error = lax.scan(visit, jnp.zeros((D, FF), jnp.float32), (tokens, upstream, worker_error))
    average = running / N_GRP + server_error
    owner = compress(average)
    return (owner.astype(jnp.bfloat16), new_worker_error, average - owner)
```

```python
import functools

import jax
import jax.numpy as jnp
from jax import lax
from jax.experimental import pallas as pl
from jax.experimental.pallas import tpu as pltpu
from jax.sharding import PartitionSpec as P

DECAY_RATE = 0.9
LINEAR_SPAN = 0.0625
EPSILON = 1e-06
MESH = pl.DeviceIdType.MESH

NX, NY, NZ = 4, 4, 8
GROUPS = 8
ROWS = 64
SIDE = 384
PIECE = 128
PIECES = 12
HEAD = 16
STEP = 32
HALF = SIDE // 2

FIRST_MM = 9
RELAY = 8


def done_pieces(tick):
    return max(0, min(2 * (tick - FIRST_MM + 1), tick - 4, PIECES))


def done_stretches(tick):
    return (2 * done_pieces(tick - 1)) // 3


def first_tick(predicate):
    return next(tick for tick in range(100) if predicate(tick))


OWN_0 = first_tick(lambda t: done_stretches(t - 1) >= 4)
OWN_1 = first_tick(lambda t: done_stretches(t - 1) >= 8)
TICKS = OWN_1 + 4


def traced_pieces(tick):
    return jnp.maximum(0, jnp.minimum(jnp.minimum(2 * (tick - FIRST_MM + 1), tick - 4), PIECES))


def traced_stretches(tick):
    return (2 * traced_pieces(tick - 1)) // 3


def stretch_of(y, core, c):
    hop = c + 1
    forward = lax.rem(y + hop, 4)
    backward = lax.rem(y + 3 * hop, 4)
    return 2 * jnp.where(core == 0, forward, backward) + c // 4


def kernel(
    tok_ref, up_ref, mom_ref, we_ref, se_ref,
    nm_out, nwe_out, nse_out,
    tok_a, tok_b, up_a, up_b, grads, sent_own, sent_far, mom, we, nwe, lev, got, nm, se, work, nse,
    s_in, s_send, s_dist, s_ax, s_az, s_bx, s_bz, s_up, s_far, s_relay, s_grad, s_lev, s_nm, s_half, s_out,
):
    grp = lax.axis_index("grp")
    rep = lax.axis_index("rep")
    y, j = grp // 2, lax.rem(grp, 2)
    x, z = rep // NZ, lax.rem(rep, NZ)
    h = x // 2
    q = lax.rem((x + 1) // 2, 2)
    x_in = x + 1 - 2 * lax.rem(x, 2)
    x_far = 3 - x
    z_up, z_down = lax.rem(z + 1, NZ), lax.rem(z + NZ - 1, NZ)
    y_up, y_down = lax.rem(y + 1, NY), lax.rem(y + NY - 1, NY)
    home = j == h

    def device(xx, yy, zz, core):
        return (2 * yy + core, NZ * xx + zz)

    inner = device(x_in, y, z, j)
    above = device(x, y, z_up, j)
    below = device(x, y, z_down, j)
    sibling = device(x, y, z, 1 - j)

    def remote(src, dst, sem, target):
        pltpu.make_async_remote_copy(
            src_ref=src, dst_ref=dst, send_sem=s_send, recv_sem=sem, device_id=target, device_id_type=MESH
        ).start()

    def local(src, dst, sem):
        pltpu.make_async_copy(src, dst, sem).start()

    def wait(ref, sem):
        pltpu.make_async_copy(ref, ref, sem).wait()

    barrier = pltpu.get_barrier_semaphore()
    greeted = [inner, above, below, device(x_far, y, z, 0), device(x_far, y, z, 1), sibling]
    for hop in range(1, NY):
        for core in range(2):
            greeted.append(device(x, lax.rem(y + hop, NY), z, core))
    for target in greeted:
        pl.semaphore_signal(barrier, inc=1, device_id=target, device_id_type=MESH)
    pl.semaphore_wait(barrier, len(greeted))

    near_x = jnp.where(home, x, x_far)

    def distribute(i, carry):
        for core in range(2):
            piece = 2 * i + core
            column = stretch_of(y, j, piece // 3) * SIDE + lax.rem(piece, 3) * PIECE
            src = tok_ref.at[:, pl.ds(pl.multiple_of(column, PIECE), PIECE)]
            for half in range(2):
                dst = tok_a.at[i, z, q] if half == 0 else tok_b.at[i, q, z]
                sem = s_dist.at[i, half]
                if core == half:

                    @pl.when((h == half) & home)
                    def _():
                        local(src, dst, sem)

                    @pl.when((h == half) & jnp.logical_not(home))
                    def _():
                        remote(src, dst, sem, device(x_far, y, z, core))
                else:

                    @pl.when(h == half)
                    def _():
                        remote(src, dst, sem, device(near_x, y, z, core))

        return carry

    lax.fori_loop(0, PIECES, distribute, 0)

    @pl.when(home)
    def _():
        for k in range(2):
            local(up_ref.at[k], up_a.at[0, :, k], s_up.at[k])
            local(up_ref.at[3 - k], up_b.at[0, k], s_up.at[2 + k])
        for k in range(2):
            remote(up_ref.at[k], up_a.at[0, :, k], s_up.at[k], sibling)
            remote(up_ref.at[3 - k], up_b.at[0, k], s_up.at[2 + k], sibling)

    @pl.when(jnp.logical_not(home))
    def _():
        for k in range(2):
            remote(up_ref.at[k], up_a.at[1, :, k], s_far.at[0], device(x_far, y, z, k))
            remote(up_ref.at[3 - k], up_b.at[1, k], s_far.at[1], device(x_far, y, z, k))

    local(mom_ref, mom, s_in.at[0])
    local(we_ref, we, s_in.at[1])
    local(se_ref, se, s_in.at[2])

    z_at = lambda d: lax.rem(z + d + NZ, NZ)

    def matmul(i, carry):
        left_a = tok_a[i].reshape(16 * ROWS, PIECE)
        left_b = tok_b[i].reshape(16 * ROWS, PIECE)
        contract = (((0,), (0,)), ((), ()))
        piece = 2 * i + j

        def product(slot):
            one = lax.dot_general(left_a, up_a[slot].reshape(16 * ROWS, SIDE), contract, preferred_element_type=jnp.float32)
            two = lax.dot_general(left_b, up_b[slot].reshape(16 * ROWS, SIDE), contract, preferred_element_type=jnp.float32)
            return (one + two).astype(jnp.bfloat16)

        sent_far[i] = product(1)
        remote(sent_far.at[i], grads.at[piece], s_grad.at[piece], device(x_far, y, z, h))
        own = product(0)

        @pl.when(home)
        def _():
            grads[piece] = own

        @pl.when(jnp.logical_not(home))
        def _():
            sent_own[i] = own
            remote(sent_own.at[i], grads.at[piece], s_grad.at[piece], sibling)

        return carry

    def scale_of(total):
        energy = jnp.sum(jnp.sum(total, axis=0, keepdims=True), axis=1, keepdims=True) * (1.0 / (SIDE * SIDE))
        scale = jnp.sqrt(energy + EPSILON).astype(jnp.bfloat16)
        return scale, scale.astype(jnp.float32)

    def compress(c, carry):
        at = stretch_of(y, j, c)
        total = jnp.zeros((STEP, SIDE), jnp.float32)
        for m in range(3):
            piece = 3 * c + m

            @pl.when(jnp.logical_not(home & (lax.rem(piece, 2) == j)))
            def _():
                wait(grads.at[piece], s_grad.at[piece])

            def add(n, total, m=m, piece=piece):
                row = n * STEP
                rows = pl.ds(pl.multiple_of(m * PIECE + row, STEP), STEP)
                value = (
                    DECAY_RATE * mom[at, rows].astype(jnp.float32)
                    + (1.0 - DECAY_RATE) * grads[piece, pl.ds(pl.multiple_of(row, STEP), STEP)].astype(jnp.float32)
                    + we[at, rows].astype(jnp.float32)
                )
                work[rows] = value
                return total + value * value

            total = lax.fori_loop(0, PIECE // STEP, add, total)
        scale, wide = scale_of(total)
        inverse = 1.0 / (LINEAR_SPAN * wide)
        lev[c, pl.ds(SIDE, HEAD)] = jnp.broadcast_to(scale, (HEAD, SIDE))

        def code(n, carry):
            rows = pl.ds(pl.multiple_of(n * STEP, STEP), STEP)
            value = work[rows]
            level = jnp.clip(value * inverse, -1.0, 1.0).astype(jnp.bfloat16)
            lev[c, rows] = level
            nwe[c, rows] = (value - wide * level.astype(jnp.float32)).astype(jnp.bfloat16)
            return carry

        lax.fori_loop(0, SIDE // STEP, code, 0)
        mine = at == grp

        @pl.when(mine)
        def _():
            local(lev.at[c], got.at[grp], s_lev.at[grp])

        @pl.when(jnp.logical_not(mine))
        def _():
            remote(lev.at[c], got.at[grp], s_lev.at[grp], (at, rep))

        local(nwe.at[c], nwe_out.at[at], s_out.at[0])
        return carry

    def own():
        for k in range(GROUPS):
            wait(got.at[k], s_lev.at[k])
        scales = [got[k, pl.ds(SIDE, HEAD)][0:1].astype(jnp.float32) for k in range(GROUPS)]

        def add(n, total):
            rows = pl.ds(pl.multiple_of(n * STEP, STEP), STEP)
            value = scales[0] * got[0, rows].astype(jnp.float32)
            for k in range(1, GROUPS):
                value += scales[k] * got[k, rows].astype(jnp.float32)
            value = value * (1.0 / GROUPS) + se[rows]
            work[rows] = value
            return total + value * value

        total = lax.fori_loop(0, SIDE // STEP, add, jnp.zeros((STEP, SIDE), jnp.float32))
        scale, wide = scale_of(total)
        inverse = 1.0 / (LINEAR_SPAN * wide)

        def code(n, carry):
            rows = pl.ds(pl.multiple_of(n * STEP, STEP), STEP)
            value = work[rows]
            level = jnp.clip(value * inverse, -1.0, 1.0).astype(jnp.bfloat16)
            decoded = wide * level.astype(jnp.float32)
            nm[grp, rows] = decoded.astype(jnp.bfloat16)
            nse[rows] = value - decoded
            return carry

        lax.fori_loop(0, SIDE // STEP, code, 0)
        block = nm.at[grp]
        remote(block, block, s_nm.at[grp], device(x, y_up, z, j))
        remote(block, block, s_nm.at[grp], device(x, y_down, z, j))
        remote(block, block, s_nm.at[grp], sibling)
        local(block, nm_out.at[grp], s_out.at[1])
        local(nse, nse_out, s_out.at[2])

    def spread_near():
        top, bottom = pl.ds(0, HALF), pl.ds(HALF, HALF)
        for yy, target, rows, which in ((y_down, y_up, top, 0), (y_up, y_down, bottom, 1)):
            at = 2 * yy + j
            wait(nm.at[at], s_nm.at[at])
            remote(nm.at[at, rows], nm.at[at, rows], s_half.at[which], device(x, target, z, j))
            remote(nm.at[at], nm.at[at], s_nm.at[at], sibling)
            local(nm.at[at], nm_out.at[at], s_out.at[1])

    def spread_far():
        at = 2 * lax.rem(y + 2, NY) + j
        wait(nm.at[at, pl.ds(0, HALF)], s_half.at[0])
        wait(nm.at[at, pl.ds(HALF, HALF)], s_half.at[1])
        remote(nm.at[at], nm.at[at], s_nm.at[at], sibling)
        local(nm.at[at], nm_out.at[at], s_out.at[1])

    def take(core):
        for hop in (0, 1, 3, 2):
            at = 2 * lax.rem(y + hop, NY) + core
            wait(nm.at[at], s_nm.at[at])
            local(nm.at[at], nm_out.at[at], s_out.at[1])

    def tick(t, carry):
        def stage(s):
            i = t - s
            return i, (i >= 0) & (i < PIECES)

        i0, on = stage(0)

        @pl.when(on)
        def _():
            i = i0
            wait(tok_a.at[i, z, q], s_dist.at[i, 0])
            block = tok_a.at[i, z, q]
            remote(block, block, s_ax.at[i], inner)
            wait(tok_b.at[i, q, z], s_dist.at[i, 1])
            block = tok_b.at[i, q, z]
            remote(block, block, s_bz.at[i, 0, 0], above)
            remote(block, block, s_bz.at[i, 0, 1], below)
            remote(block, block, s_bx.at[i], inner)

        for s in range(1, 6):
            i_s, on = stage(s)

            @pl.when(on)
            def _(i=i_s, s=s):
                if s == 1:
                    wait(tok_a.at[i, z, 1 - q], s_ax.at[i])
                    block = tok_a.at[i, z]
                    remote(block, block, s_az.at[i, 0, 0], above)
                    remote(block, block, s_az.at[i, 0, 1], below)
                elif s <= 3:
                    for way, sign, target in ((0, -1, above), (1, 1, below)):
                        block = tok_a.at[i, z_at(sign * (s - 1))]
                        wait(block, s_az.at[i, s - 2, way])
                        remote(block, block, s_az.at[i, s - 1, way], target)
                elif s == 4:
                    for way, sign, target in ((0, -1, above), (1, 1, below)):
                        block = tok_a.at[i, z_at(sign * 3)]
                        wait(block, s_az.at[i, 2, way])
                        part = tok_a.at[i, z_at(sign * 3), way]
                        remote(part, part, s_az.at[i, 3, way], target)
                else:
                    for way in range(2):
                        wait(tok_a.at[i, z_at(4), way], s_az.at[i, 3, way])
                if s <= 2:
                    for way, sign, target in ((0, -1, above), (1, 1, below)):
                        block = tok_b.at[i, q, z_at(sign * s)]
                        wait(block, s_bz.at[i, s - 1, way])
                        remote(block, block, s_bz.at[i, s, way], target)
                        remote(block, block, s_bx.at[i], inner)
                elif s == 3:
                    for way, sign, target in ((0, -1, above), (1, 1, below)):
                        block = tok_b.at[i, q, z_at(sign * 3)]
                        wait(block, s_bz.at[i, 2, way])
                        part = tok_b.at[i, q, z_at(sign * 3), pl.ds(32 * way, 32)]
                        remote(part, part, s_bz.at[i, 3, way], target)
                        remote(block, block, s_bx.at[i], inner)
                elif s == 4:
                    for way in range(2):
                        wait(tok_b.at[i, q, z_at(4), pl.ds(32 * way, 32)], s_bz.at[i, 3, way])
                    block = tok_b.at[i, q, z_at(4)]
                    remote(block, block, s_bx.at[i], inner)
                else:
                    wait(tok_b.at[i, 1 - q], s_bx.at[i])

        @pl.when(t == RELAY)
        def _():
            block = up_a.at[1, :, j]
            wait(block, s_far.at[0])
            remote(block, block, s_relay.at[0], sibling)
            block = up_b.at[1, j]
            wait(block, s_far.at[1])
            remote(block, block, s_relay.at[1], sibling)

        @pl.when(t == FIRST_MM)
        def _():
            for k in range(2):
                wait(up_a.at[0, :, k], s_up.at[k])
                wait(up_b.at[0, k], s_up.at[2 + k])
            wait(up_a.at[1, :, 1 - j], s_relay.at[0])
            wait(up_b.at[1, 1 - j], s_relay.at[1])
            wait(mom, s_in.at[0])
            wait(we, s_in.at[1])
            wait(se, s_in.at[2])

        lax.fori_loop(traced_pieces(t - 1), traced_pieces(t), matmul, 0)
        lax.fori_loop(traced_stretches(t - 1), traced_stretches(t), compress, 0)

        pl.when(t == jnp.where(j == 0, OWN_0, OWN_1))(own)
        pl.when(t == jnp.where(j == 0, OWN_0, OWN_1) + 1)(spread_near)
        pl.when(t == jnp.where(j == 0, OWN_0, OWN_1) + 2)(spread_far)

        @pl.when(t == jnp.where(j == 0, OWN_1, OWN_0) + 3)
        def _():
            take(1 - j)

        return carry

    lax.fori_loop(0, TICKS, tick, 0)

    for i in range(PIECES):
        pass

    def drain(i, carry):
        wait(tok_a.at[i], s_send)
        wait(tok_b.at[i, 0], s_send)
        wait(tok_b.at[i, 1, pl.ds(0, 6)], s_send)
        wait(sent_far.at[i], s_send)

        @pl.when(jnp.logical_not(home))
        def _():
            wait(sent_own.at[i], s_send)
            wait(tok_a.at[i, 0], s_send)

        @pl.when(home)
        def _():
            wait(tok_a.at[i, 0, 0], s_send)

        return carry

    lax.fori_loop(0, PIECES, drain, 0)
    wait(up_ref, s_send)
    wait(up_a.at[1, :, 0], s_send)
    wait(up_b.at[1, 0], s_send)

    def drain_levels(c, carry):
        @pl.when(stretch_of(y, j, c) != grp)
        def _():
            wait(lev.at[c], s_send)

        return carry

    lax.fori_loop(0, GROUPS, drain_levels, 0)
    for _ in range(7):
        wait(nm.at[0], s_send)
    wait(nwe, s_out.at[0])
    wait(nm, s_out.at[1])
    wait(nse, s_out.at[2])


def body(tokens, upstream, momentum, worker_error, server_error):
    bf16, f32 = jnp.bfloat16, jnp.float32
    anywhere = pl.BlockSpec(memory_space=pl.ANY)
    dma = pltpu.SemaphoreType.DMA
    stretches = (GROUPS, SIDE, SIDE)
    new_momentum, new_worker_error, new_server_error = pl.pallas_call(
        kernel,
        out_shape=(
            jax.ShapeDtypeStruct(stretches, bf16),
            jax.ShapeDtypeStruct(stretches, bf16),
            jax.ShapeDtypeStruct((SIDE, SIDE), f32),
        ),
        in_specs=[anywhere] * 5,
        out_specs=[anywhere] * 3,
        scratch_shapes=[
            pltpu.VMEM((PIECES, NZ, 2, ROWS, PIECE), bf16),
            pltpu.VMEM((PIECES, 2, NZ, ROWS, PIECE), bf16),
            pltpu.VMEM((2, NZ, 2, ROWS, SIDE), bf16),
            pltpu.VMEM((2, 2, NZ, ROWS, SIDE), bf16),
            pltpu.VMEM((2 * PIECES, PIECE, SIDE), bf16),
            pltpu.VMEM((PIECES, PIECE, SIDE), bf16),
            pltpu.VMEM((PIECES, PIECE, SIDE), bf16),
            pltpu.VMEM(stretches, bf16),
            pltpu.VMEM(stretches, bf16),
            pltpu.VMEM(stretches, bf16),
            pltpu.VMEM((GROUPS, SIDE + HEAD, SIDE), bf16),
            pltpu.VMEM((GROUPS, SIDE + HEAD, SIDE), bf16),
            pltpu.VMEM(stretches, bf16),
            pltpu.VMEM((SIDE, SIDE), f32),
            pltpu.VMEM((SIDE, SIDE), f32),
            pltpu.VMEM((SIDE, SIDE), f32),
            dma((3,)),
            dma,
            dma((PIECES, 2)),
            dma((PIECES,)),
            dma((PIECES, 4, 2)),
            dma((PIECES,)),
            dma((PIECES, 4, 2)),
            dma((4,)),
            dma((2,)),
            dma((2,)),
            dma((2 * PIECES,)),
            dma((GROUPS,)),
            dma((GROUPS,)),
            dma((2,)),
            dma((3,)),
        ],
        name="compressed_step",
        compiler_params=pltpu.CompilerParams(
            collective_id=0, has_side_effects=True, vmem_limit_bytes=48 * 1024 * 1024
        ),
    )(
        tokens[0],
        upstream[0].reshape(NX, NZ, ROWS, SIDE),
        momentum.reshape(stretches),
        worker_error[0].reshape(stretches),
        server_error,
    )
    return (
        new_momentum.reshape(GROUPS * SIDE, SIDE),
        new_worker_error.reshape(1, GROUPS * SIDE, SIDE),
        new_server_error,
    )


def solution(mesh):
    placed = (
        P("grp", "rep", None),
        P("grp", None, "rep"),
        P(None, "rep"),
        P("grp", None, "rep"),
        P("grp", "rep"),
    )
    return jax.shard_map(
        body,
        mesh=mesh,
        in_specs=placed,
        out_specs=(P(None, "rep"), P("grp", None, "rep"), P("grp", "rep")),
        check_vma=False,
    )
```

```python
import functools

import jax
import jax.numpy as jnp
from jax import lax
from jax.experimental import pallas as pl
from jax.experimental.pallas import tpu as pltpu
from jax.sharding import PartitionSpec as P

DECAY_RATE = 0.9
LINEAR_SPAN = 0.0625
EPSILON = 1e-06
MESH = pl.DeviceIdType.MESH

NX, NY, NZ = 4, 4, 8
GROUPS = 8
ROWS = 64
SIDE = 384
PIECE = 128
PIECES = 12
HEAD = 16
STEP = 32
HALF = SIDE // 2

AHEAD = 1
FIRST_MM = 7
RELAY = 6
LAG = 2
LATE = 16
OWN = (16, 17)
NEAR = (17, 18)
FAR = (18, 19)
TAKE = (19, 20)
TICKS = 21
DRAIN = 17
EARLY = 7


def entered(tick):
    return jnp.where(tick < 0, 0, jnp.minimum(tick + 1 + AHEAD, PIECES))


def done_pieces(tick):
    return jnp.maximum(0, jnp.minimum(2 * (tick - FIRST_MM + 1), entered(tick - 5)))


def done_stretches(tick):
    return (2 * done_pieces(tick - jnp.where(tick < LATE, LAG, 1))) // 3


def stretch_of(y, core, c):
    pair = c // 2
    hop = jnp.where(pair == 0, 2, jnp.where(pair == 3, 0, jnp.where((pair == 1) == (core == 0), 1, 3)))
    return 2 * lax.rem(y + hop, NY) + lax.rem(c, 2)


def kernel(
    tok_ref, up_ref, mom_ref, we_ref, se_ref,
    nm_out, nwe_out, nse_out,
    tok_a, tok_b, up_a, up_b, grads, sent_own, sent_far, mom, we, nwe, lev, got, nm, se, work, nse,
    s_in, s_send, s_dist, s_ax, s_az, s_bx, s_bz, s_up, s_far, s_relay, s_grad, s_lev, s_nm, s_half, s_out,
):
    grp = lax.axis_index("grp")
    rep = lax.axis_index("rep")
    y, j = grp // 2, lax.rem(grp, 2)
    x, z = rep // NZ, lax.rem(rep, NZ)
    h = x // 2
    q = lax.rem((x + 1) // 2, 2)
    x_in = x + 1 - 2 * lax.rem(x, 2)
    x_far = 3 - x
    z_up, z_down = lax.rem(z + 1, NZ), lax.rem(z + NZ - 1, NZ)
    y_up, y_down = lax.rem(y + 1, NY), lax.rem(y + NY - 1, NY)
    home = j == h

    def device(xx, yy, zz, core):
        return (2 * yy + core, NZ * xx + zz)

    inner = device(x_in, y, z, j)
    above = device(x, y, z_up, j)
    below = device(x, y, z_down, j)
    sibling = device(x, y, z, 1 - j)

    def remote(src, dst, sem, target):
        pltpu.make_async_remote_copy(
            src_ref=src, dst_ref=dst, send_sem=s_send, recv_sem=sem, device_id=target, device_id_type=MESH
        ).start()

    def local(src, dst, sem):
        pltpu.make_async_copy(src, dst, sem).start()

    def wait(ref, sem):
        pltpu.make_async_copy(ref, ref, sem).wait()

    barrier = pltpu.get_barrier_semaphore()
    greeted = [inner, above, below, device(x_far, y, z, 0), device(x_far, y, z, 1), sibling]
    for hop in range(1, NY):
        for core in range(2):
            greeted.append(device(x, lax.rem(y + hop, NY), z, core))
    for target in greeted:
        pl.semaphore_signal(barrier, inc=1, device_id=target, device_id_type=MESH)
    pl.semaphore_wait(barrier, len(greeted))

    near_x = jnp.where(home, x, x_far)

    def distribute(i, carry):
        for core in range(2):
            piece = 2 * i + core
            column = stretch_of(y, j, piece // 3) * SIDE + lax.rem(piece, 3) * PIECE
            src = tok_ref.at[:, pl.ds(pl.multiple_of(column, PIECE), PIECE)]
            for half in range(2):
                dst = tok_a.at[i, z, q] if half == 0 else tok_b.at[i, q, z]
                sem = s_dist.at[i, half]
                if core == half:

                    @pl.when((h == half) & home)
                    def _():
                        local(src, dst, sem)

                    @pl.when((h == half) & jnp.logical_not(home))
                    def _():
                        remote(src, dst, sem, device(x_far, y, z, core))
                else:

                    @pl.when(h == half)
                    def _():
                        remote(src, dst, sem, device(near_x, y, z, core))

        return carry

    lax.fori_loop(0, EARLY, distribute, 0)

    @pl.when(home)
    def _():
        for k in range(2):
            local(up_ref.at[k], up_a.at[0, :, k], s_up.at[k])
            local(up_ref.at[3 - k], up_b.at[0, k], s_up.at[2 + k])
        for k in range(2):
            remote(up_ref.at[k], up_a.at[0, :, k], s_up.at[k], sibling)
            remote(up_ref.at[3 - k], up_b.at[0, k], s_up.at[2 + k], sibling)

    @pl.when(jnp.logical_not(home))
    def _():
        for k in range(2):
            remote(up_ref.at[k], up_a.at[1, :, k], s_far.at[0], device(x_far, y, z, k))
            remote(up_ref.at[3 - k], up_b.at[1, k], s_far.at[1], device(x_far, y, z, k))

    lax.fori_loop(EARLY, PIECES, distribute, 0)
    local(mom_ref, mom, s_in.at[0])
    local(we_ref, we, s_in.at[1])
    local(se_ref, se, s_in.at[2])

    z_at = lambda d: lax.rem(z + d + NZ, NZ)

    def matmul(i, carry):
        left_a = tok_a[i].reshape(16 * ROWS, PIECE)
        left_b = tok_b[i].reshape(16 * ROWS, PIECE)
        contract = (((0,), (0,)), ((), ()))
        piece = 2 * i + j

        def product(slot):
            one = lax.dot_general(left_a, up_a[slot].reshape(16 * ROWS, SIDE), contract, preferred_element_type=jnp.float32)
            two = lax.dot_general(left_b, up_b[slot].reshape(16 * ROWS, SIDE), contract, preferred_element_type=jnp.float32)
            return (one + two).astype(jnp.bfloat16)

        sent_far[i] = product(1)
        remote(sent_far.at[i], grads.at[piece], s_grad.at[piece], device(x_far, y, z, h))
        own = product(0)

        @pl.when(home)
        def _():
            grads[piece] = own

        @pl.when(jnp.logical_not(home))
        def _():
            sent_own[i] = own
            remote(sent_own.at[i], grads.at[piece], s_grad.at[piece], sibling)

        return carry

    def scale_of(total):
        energy = jnp.sum(jnp.sum(total, axis=0, keepdims=True), axis=1, keepdims=True) * (1.0 / (SIDE * SIDE))
        scale = jnp.sqrt(energy + EPSILON).astype(jnp.bfloat16)
        return scale, scale.astype(jnp.float32)

    def compress(c, carry):
        at = stretch_of(y, j, c)
        total = jnp.zeros((STEP, SIDE), jnp.float32)
        for m in range(3):
            piece = 3 * c + m

            @pl.when(jnp.logical_not(home & (lax.rem(piece, 2) == j)))
            def _():
                wait(grads.at[piece], s_grad.at[piece])

            def add(n, total, m=m, piece=piece):
                row = n * STEP
                rows = pl.ds(pl.multiple_of(m * PIECE + row, STEP), STEP)
                value = (
                    DECAY_RATE * mom[at, rows].astype(jnp.float32)
                    + (1.0 - DECAY_RATE) * grads[piece, pl.ds(pl.multiple_of(row, STEP), STEP)].astype(jnp.float32)
                    + we[at, rows].astype(jnp.float32)
                )
                work[rows] = value
                return total + value * value

            total = lax.fori_loop(0, PIECE // STEP, add, total, unroll=True)
        scale, wide = scale_of(total)
        inverse = 1.0 / (LINEAR_SPAN * wide)
        lev[c, pl.ds(SIDE, HEAD)] = jnp.broadcast_to(scale, (HEAD, SIDE))

        def code(n, carry):
            rows = pl.ds(pl.multiple_of(n * STEP, STEP), STEP)
            value = work[rows]
            level = jnp.clip(value * inverse, -1.0, 1.0).astype(jnp.bfloat16)
            lev[c, rows] = level
            nwe[c, rows] = (value - wide * level.astype(jnp.float32)).astype(jnp.bfloat16)
            return carry

        lax.fori_loop(0, SIDE // STEP, code, 0, unroll=True)
        mine = at == grp

        @pl.when(mine)
        def _():
            local(lev.at[c], got.at[grp], s_lev.at[grp])

        @pl.when(jnp.logical_not(mine))
        def _():
            remote(lev.at[c], got.at[grp], s_lev.at[grp], (at, rep))

        local(nwe.at[c], nwe_out.at[at], s_out.at[0])
        return carry

    def own():
        for k in range(GROUPS):
            wait(got.at[k], s_lev.at[k])
        scales = [got[k, pl.ds(SIDE, HEAD)][0:1].astype(jnp.float32) for k in range(GROUPS)]

        def add(n, total):
            rows = pl.ds(pl.multiple_of(n * STEP, STEP), STEP)
            value = scales[0] * got[0, rows].astype(jnp.float32)
            for k in range(1, GROUPS):
                value += scales[k] * got[k, rows].astype(jnp.float32)
            value = value * (1.0 / GROUPS) + se[rows]
            work[rows] = value
            return total + value * value

        total = lax.fori_loop(0, SIDE // STEP, add, jnp.zeros((STEP, SIDE), jnp.float32), unroll=True)
        scale, wide = scale_of(total)
        inverse = 1.0 / (LINEAR_SPAN * wide)

        def code(n, carry):
            rows = pl.ds(pl.multiple_of(n * STEP, STEP), STEP)
            value = work[rows]
            level = jnp.clip(value * inverse, -1.0, 1.0).astype(jnp.bfloat16)
            decoded = wide * level.astype(jnp.float32)
            nm[grp, rows] = decoded.astype(jnp.bfloat16)
            nse[rows] = value - decoded
            return carry

        lax.fori_loop(0, SIDE // STEP, code, 0, unroll=True)
        block = nm.at[grp]
        remote(block, block, s_nm.at[grp], device(x, y_up, z, j))
        remote(block, block, s_nm.at[grp], device(x, y_down, z, j))
        remote(block, block, s_nm.at[grp], sibling)
        local(block, nm_out.at[grp], s_out.at[1])
        local(nse, nse_out, s_out.at[2])

    def spread_near():
        top, bottom = pl.ds(0, HALF), pl.ds(HALF, HALF)
        for yy, target, rows, which in ((y_down, y_up, top, 0), (y_up, y_down, bottom, 1)):
            at = 2 * yy + j
            wait(nm.at[at], s_nm.at[at])
            remote(nm.at[at, rows], nm.at[at, rows], s_half.at[which], device(x, target, z, j))
            remote(nm.at[at], nm.at[at], s_nm.at[at], sibling)
            local(nm.at[at], nm_out.at[at], s_out.at[1])

    def spread_far():
        at = 2 * lax.rem(y + 2, NY) + j
        wait(nm.at[at, pl.ds(0, HALF)], s_half.at[0])
        wait(nm.at[at, pl.ds(HALF, HALF)], s_half.at[1])
        remote(nm.at[at], nm.at[at], s_nm.at[at], sibling)
        local(nm.at[at], nm_out.at[at], s_out.at[1])

    def take(core):
        for hop in (0, 1, 3, 2):
            at = 2 * lax.rem(y + hop, NY) + core
            wait(nm.at[at], s_nm.at[at])
            local(nm.at[at], nm_out.at[at], s_out.at[1])

    def drain_levels(c, carry):
        @pl.when(stretch_of(y, j, c) != grp)
        def _():
            wait(lev.at[c], s_send)

        return carry

    def drain(i, carry):
        wait(tok_a.at[i], s_send)
        wait(tok_b.at[i, 0], s_send)
        wait(tok_b.at[i, 1, pl.ds(0, 6)], s_send)
        wait(sent_far.at[i], s_send)

        @pl.when(jnp.logical_not(home))
        def _():
            wait(sent_own.at[i], s_send)
            wait(tok_a.at[i, 0], s_send)

        @pl.when(home)
        def _():
            wait(tok_a.at[i, 0, 0], s_send)

        return carry

    def drain_gather():
        lax.fori_loop(0, PIECES, drain, 0)
        wait(up_ref, s_send)
        wait(up_a.at[1, :, 0], s_send)
        wait(up_b.at[1, 0], s_send)
        lax.fori_loop(0, GROUPS, drain_levels, 0)

    def stage(s, i, carry):
        if s == 0:
            block = tok_a.at[i, z, q]
            wait(block, s_dist.at[i, 0])
            remote(block, block, s_ax.at[i], inner)
            block = tok_b.at[i, q, z]
            wait(block, s_dist.at[i, 1])
            remote(block, block, s_bz.at[i, 0, 0], above)
            remote(block, block, s_bz.at[i, 0, 1], below)
            remote(block, block, s_bx.at[i], inner)
        else:
            if s == 1:
                wait(tok_a.at[i, z, 1 - q], s_ax.at[i])
                block = tok_a.at[i, z]
                remote(block, block, s_az.at[i, 0, 0], above)
                remote(block, block, s_az.at[i, 0, 1], below)
            elif s <= 3:
                for way, sign, target in ((0, -1, above), (1, 1, below)):
                    block = tok_a.at[i, z_at(sign * (s - 1))]
                    wait(block, s_az.at[i, s - 2, way])
                    remote(block, block, s_az.at[i, s - 1, way], target)
            elif s == 4:
                for way, sign, target in ((0, -1, above), (1, 1, below)):
                    block = tok_a.at[i, z_at(sign * 3)]
                    wait(block, s_az.at[i, 2, way])
                    part = tok_a.at[i, z_at(sign * 3), way]
                    remote(part, part, s_az.at[i, 3, way], target)
            else:
                for way in range(2):
                    wait(tok_a.at[i, z_at(4), way], s_az.at[i, 3, way])
            if s <= 2:
                for way, sign, target in ((0, -1, above), (1, 1, below)):
                    block = tok_b.at[i, q, z_at(sign * s)]
                    wait(block, s_bz.at[i, s - 1, way])
                    remote(block, block, s_bz.at[i, s, way], target)
                    remote(block, block, s_bx.at[i], inner)
            elif s == 3:
                for way, sign, target in ((0, -1, above), (1, 1, below)):
                    block = tok_b.at[i, q, z_at(sign * 3)]
                    wait(block, s_bz.at[i, 2, way])
                    part = tok_b.at[i, q, z_at(sign * 3), pl.ds(32 * way, 32)]
                    remote(part, part, s_bz.at[i, 3, way], target)
                    remote(block, block, s_bx.at[i], inner)
            elif s == 4:
                for way in range(2):
                    wait(tok_b.at[i, q, z_at(4), pl.ds(32 * way, 32)], s_bz.at[i, 3, way])
                block = tok_b.at[i, q, z_at(4)]
                remote(block, block, s_bx.at[i], inner)
            else:
                wait(tok_b.at[i, 1 - q], s_bx.at[i])
        return carry

    def tick(t, carry):
        for s in range(6):
            lax.fori_loop(entered(t - s - 1), entered(t - s), functools.partial(stage, s), 0)

        @pl.when(t == RELAY)
        def _():
            block = up_a.at[1, :, j]
            wait(block, s_far.at[0])
            remote(block, block, s_relay.at[0], sibling)
            block = up_b.at[1, j]
            wait(block, s_far.at[1])
            remote(block, block, s_relay.at[1], sibling)

        @pl.when(t == FIRST_MM)
        def _():
            for k in range(2):
                wait(up_a.at[0, :, k], s_up.at[k])
                wait(up_b.at[0, k], s_up.at[2 + k])
            wait(up_a.at[1, :, 1 - j], s_relay.at[0])
            wait(up_b.at[1, 1 - j], s_relay.at[1])
            wait(mom, s_in.at[0])
            wait(we, s_in.at[1])
            wait(se, s_in.at[2])

        lax.fori_loop(done_pieces(t - 1), done_pieces(t), matmul, 0)
        lax.fori_loop(done_stretches(t - 1), done_stretches(t), compress, 0)

        pl.when(t == jnp.where(j == 0, OWN[0], OWN[1]))(own)
        pl.when(t == DRAIN)(drain_gather)
        pl.when(t == jnp.where(j == 0, NEAR[0], NEAR[1]))(spread_near)
        pl.when(t == jnp.where(j == 0, FAR[0], FAR[1]))(spread_far)

        @pl.when(t == jnp.where(j == 0, TAKE[1], TAKE[0]))
        def _():
            take(1 - j)

        return carry

    lax.fori_loop(0, TICKS, tick, 0)

    for _ in range(7):
        wait(nm.at[0], s_send)
    wait(nwe, s_out.at[0])
    wait(nm, s_out.at[1])
    wait(nse, s_out.at[2])


def tidy(nm_ref, nwe_ref, nse_ref, nm_out, nwe_out, nse_out, sems):
    pairs = ((nwe_ref, nwe_out), (nm_ref, nm_out), (nse_ref, nse_out))
    copies = [pltpu.make_async_copy(src, dst, sems.at[n]) for n, (src, dst) in enumerate(pairs)]
    for copy in copies:
        copy.start()
    for copy in copies:
        copy.wait()


def body(tokens, upstream, momentum, worker_error, server_error):
    bf16, f32 = jnp.bfloat16, jnp.float32
    anywhere = pl.BlockSpec(memory_space=pl.ANY)
    dma = pltpu.SemaphoreType.DMA
    stretches = (GROUPS, SIDE, SIDE)
    new_momentum, new_worker_error, new_server_error = pl.pallas_call(
        kernel,
        out_shape=(
            jax.ShapeDtypeStruct(stretches, bf16),
            jax.ShapeDtypeStruct(stretches, bf16),
            jax.ShapeDtypeStruct((SIDE, SIDE), f32),
        ),
        in_specs=[anywhere] * 5,
        out_specs=[anywhere] * 3,
        scratch_shapes=[
            pltpu.VMEM((PIECES, NZ, 2, ROWS, PIECE), bf16),
            pltpu.VMEM((PIECES, 2, NZ, ROWS, PIECE), bf16),
            pltpu.VMEM((2, NZ, 2, ROWS, SIDE), bf16),
            pltpu.VMEM((2, 2, NZ, ROWS, SIDE), bf16),
            pltpu.VMEM((2 * PIECES, PIECE, SIDE), bf16),
            pltpu.VMEM((PIECES, PIECE, SIDE), bf16),
            pltpu.VMEM((PIECES, PIECE, SIDE), bf16),
            pltpu.VMEM(stretches, bf16),
            pltpu.VMEM(stretches, bf16),
            pltpu.VMEM(stretches, bf16),
            pltpu.VMEM((GROUPS, SIDE + HEAD, SIDE), bf16),
            pltpu.VMEM((GROUPS, SIDE + HEAD, SIDE), bf16),
            pltpu.VMEM(stretches, bf16),
            pltpu.VMEM((SIDE, SIDE), f32),
            pltpu.VMEM((SIDE, SIDE), f32),
            pltpu.VMEM((SIDE, SIDE), f32),
            dma((3,)),
            dma,
            dma((PIECES, 2)),
            dma((PIECES,)),
            dma((PIECES, 4, 2)),
            dma((PIECES,)),
            dma((PIECES, 4, 2)),
            dma((4,)),
            dma((2,)),
            dma((2,)),
            dma((2 * PIECES,)),
            dma((GROUPS,)),
            dma((GROUPS,)),
            dma((2,)),
            dma((3,)),
        ],
        name="compressed_step",
        compiler_params=pltpu.CompilerParams(
            collective_id=0, has_side_effects=True, vmem_limit_bytes=60 * 1024 * 1024
        ),
    )(
        tokens[0],
        upstream[0].reshape(NX, NZ, ROWS, SIDE),
        momentum.reshape(stretches),
        worker_error[0].reshape(stretches),
        server_error,
    )
    new_momentum, new_worker_error, new_server_error = pl.pallas_call(
        tidy,
        out_shape=(
            jax.ShapeDtypeStruct(stretches, bf16),
            jax.ShapeDtypeStruct(stretches, bf16),
            jax.ShapeDtypeStruct((SIDE, SIDE), f32),
        ),
        in_specs=[pl.BlockSpec(memory_space=pltpu.VMEM)] * 3,
        out_specs=[anywhere] * 3,
        scratch_shapes=[dma((3,))],
        name="tidy",
    )(new_momentum, new_worker_error, new_server_error)
    return (
        new_momentum.reshape(GROUPS * SIDE, SIDE),
        new_worker_error.reshape(1, GROUPS * SIDE, SIDE),
        new_server_error,
    )


def solution(mesh):
    placed = (
        P("grp", "rep", None),
        P("grp", None, "rep"),
        P(None, "rep"),
        P("grp", None, "rep"),
        P("grp", "rep"),
    )
    return jax.shard_map(
        body,
        mesh=mesh,
        in_specs=placed,
        out_specs=(P(None, "rep"), P("grp", None, "rep"), P("grp", "rep")),
        check_vma=False,
    )
```

```python
import functools

import jax
import jax.numpy as jnp
from jax import lax
from jax.experimental import pallas as pl
from jax.experimental.pallas import tpu as pltpu
from jax.sharding import PartitionSpec as P

DECAY_RATE = 0.9
LINEAR_SPAN = 0.0625
EPSILON = 1e-06
MESH = pl.DeviceIdType.MESH

NX, NY, NZ = 4, 4, 8
GROUPS = 8
ROWS = 64
SIDE = 384
PIECE = 128
PIECES = 12
HEAD = 16
STEP = 32
HALF = SIDE // 2

AHEAD = 1
FIRST_MM = 7
RELAY = 6
LAG = 2
LATE = 20
OWN = (16, 17)
NEAR = (17, 18)
FAR = (18, 19)
TAKE = (19, 20)
TICKS = 21
DRAIN = 17
UP_AT = 3
LOAD_AT = 5
EARLY = 7


def entered(tick):
    return jnp.where(tick < 0, 0, jnp.minimum(tick + 1 + AHEAD, PIECES))


def done_pieces(tick):
    return jnp.maximum(0, jnp.minimum(2 * (tick - FIRST_MM + 1), entered(tick - 5)))


def done_stretches(tick):
    return (2 * done_pieces(tick - jnp.where(tick < LATE, LAG, 1))) // 3


def stretch_of(y, core, c):
    pair = c // 2
    hop = jnp.where(pair == 0, 2, jnp.where(pair == 3, 0, jnp.where((pair == 1) == (core == 0), 1, 3)))
    return 2 * lax.rem(y + hop, NY) + lax.rem(c, 2)


def kernel(
    tok_ref, up_ref, mom_ref, we_ref, se_ref,
    nm_out, nwe_out, nse_out,
    tok_a, tok_b, up_a, up_b, grads, sent_own, sent_far, mom, we, nwe, lev, got, nm, se, work, nse,
    s_in, s_send, s_dist, s_ax, s_az, s_bx, s_bz, s_up, s_far, s_relay, s_grad, s_lev, s_nm, s_half, s_out,
):
    grp = lax.axis_index("grp")
    rep = lax.axis_index("rep")
    y, j = grp // 2, lax.rem(grp, 2)
    x, z = rep // NZ, lax.rem(rep, NZ)
    h = x // 2
    q = lax.rem((x + 1) // 2, 2)
    x_in = x + 1 - 2 * lax.rem(x, 2)
    x_far = 3 - x
    z_up, z_down = lax.rem(z + 1, NZ), lax.rem(z + NZ - 1, NZ)
    y_up, y_down = lax.rem(y + 1, NY), lax.rem(y + NY - 1, NY)
    home = j == h

    def device(xx, yy, zz, core):
        return (2 * yy + core, NZ * xx + zz)

    inner = device(x_in, y, z, j)
    above = device(x, y, z_up, j)
    below = device(x, y, z_down, j)
    sibling = device(x, y, z, 1 - j)

    def remote(src, dst, sem, target):
        pltpu.make_async_remote_copy(
            src_ref=src, dst_ref=dst, send_sem=s_send, recv_sem=sem, device_id=target, device_id_type=MESH
        ).start()

    def local(src, dst, sem):
        pltpu.make_async_copy(src, dst, sem).start()

    def wait(ref, sem):
        pltpu.make_async_copy(ref, ref, sem).wait()

    barrier = pltpu.get_barrier_semaphore()
    greeted = [inner, above, below, device(x_far, y, z, 0), device(x_far, y, z, 1), sibling]
    for hop in range(1, NY):
        for core in range(2):
            greeted.append(device(x, lax.rem(y + hop, NY), z, core))
    for target in greeted:
        pl.semaphore_signal(barrier, inc=1, device_id=target, device_id_type=MESH)
    pl.semaphore_wait(barrier, len(greeted))

    near_x = jnp.where(home, x, x_far)

    def distribute(i, carry):
        for core in range(2):
            piece = 2 * i + core
            column = stretch_of(y, j, piece // 3) * SIDE + lax.rem(piece, 3) * PIECE
            src = tok_ref.at[:, pl.ds(pl.multiple_of(column, PIECE), PIECE)]
            for half in range(2):
                dst = tok_a.at[i, z, q] if half == 0 else tok_b.at[i, q, z]
                sem = s_dist.at[i, half]
                if core == half:

                    @pl.when((h == half) & home)
                    def _():
                        local(src, dst, sem)

                    @pl.when((h == half) & jnp.logical_not(home))
                    def _():
                        remote(src, dst, sem, device(x_far, y, z, core))
                else:

                    @pl.when(h == half)
                    def _():
                        remote(src, dst, sem, device(near_x, y, z, core))

        return carry

    lax.fori_loop(0, EARLY, distribute, 0)

    @pl.when(jnp.logical_not(home))
    def _():
        for k in range(2):
            remote(up_ref.at[k], up_a.at[1, :, k], s_far.at[0], device(x_far, y, z, k))
            remote(up_ref.at[3 - k], up_b.at[1, k], s_far.at[1], device(x_far, y, z, k))

    lax.fori_loop(EARLY, PIECES, distribute, 0)

    z_at = lambda d: lax.rem(z + d + NZ, NZ)

    def matmul(i, carry):
        left_a = tok_a[i].reshape(16 * ROWS, PIECE)
        left_b = tok_b[i].reshape(16 * ROWS, PIECE)
        contract = (((0,), (0,)), ((), ()))
        piece = 2 * i + j

        def product(slot):
            one = lax.dot_general(left_a, up_a[slot].reshape(16 * ROWS, SIDE), contract, preferred_element_type=jnp.float32)
            two = lax.dot_general(left_b, up_b[slot].reshape(16 * ROWS, SIDE), contract, preferred_element_type=jnp.float32)
            return (one + two).astype(jnp.bfloat16)

        sent_far[i] = product(1)
        remote(sent_far.at[i], grads.at[piece], s_grad.at[piece], device(x_far, y, z, h))
        own = product(0)

        @pl.when(home)
        def _():
            grads[piece] = own

        @pl.when(jnp.logical_not(home))
        def _():
            sent_own[i] = own
            remote(sent_own.at[i], grads.at[piece], s_grad.at[piece], sibling)

        return carry

    def scale_of(total):
        energy = jnp.sum(jnp.sum(total, axis=0, keepdims=True), axis=1, keepdims=True) * (1.0 / (SIDE * SIDE))
        scale = jnp.sqrt(energy + EPSILON).astype(jnp.bfloat16)
        return scale, scale.astype(jnp.float32)

    def compress(c, carry):
        at = stretch_of(y, j, c)
        total = jnp.zeros((STEP, SIDE), jnp.float32)
        for m in range(3):
            piece = 3 * c + m

            @pl.when(jnp.logical_not(home & (lax.rem(piece, 2) == j)))
            def _():
                wait(grads.at[piece], s_grad.at[piece])

            def add(n, total, m=m, piece=piece):
                row = n * STEP
                rows = pl.ds(pl.multiple_of(m * PIECE + row, STEP), STEP)
                value = (
                    DECAY_RATE * mom[at, rows].astype(jnp.float32)
                    + (1.0 - DECAY_RATE) * grads[piece, pl.ds(pl.multiple_of(row, STEP), STEP)].astype(jnp.float32)
                    + we[at, rows].astype(jnp.float32)
                )
                work[rows] = value
                return total + value * value

            total = lax.fori_loop(0, PIECE // STEP, add, total, unroll=True)
        scale, wide = scale_of(total)
        inverse = 1.0 / (LINEAR_SPAN * wide)
        lev[c, pl.ds(SIDE, HEAD)] = jnp.broadcast_to(scale, (HEAD, SIDE))

        def code(n, carry):
            rows = pl.ds(pl.multiple_of(n * STEP, STEP), STEP)
            value = work[rows]
            level = jnp.clip(value * inverse, -1.0, 1.0).astype(jnp.bfloat16)
            lev[c, rows] = level
            nwe[c, rows] = (value - wide * level.astype(jnp.float32)).astype(jnp.bfloat16)
            return carry

        lax.fori_loop(0, SIDE // STEP, code, 0, unroll=True)
        mine = at == grp

        @pl.when(mine)
        def _():
            local(lev.at[c], got.at[grp], s_lev.at[grp])

        @pl.when(jnp.logical_not(mine))
        def _():
            remote(lev.at[c], got.at[grp], s_lev.at[grp], (at, rep))

        local(nwe.at[c], nwe_out.at[at], s_out.at[0])
        return carry

    def own():
        for k in range(GROUPS):
            wait(got.at[k], s_lev.at[k])
        scales = [got[k, pl.ds(SIDE, HEAD)][0:1].astype(jnp.float32) for k in range(GROUPS)]

        def add(n, total):
            rows = pl.ds(pl.multiple_of(n * STEP, STEP), STEP)
            value = scales[0] * got[0, rows].astype(jnp.float32)
            for k in range(1, GROUPS):
                value += scales[k] * got[k, rows].astype(jnp.float32)
            value = value * (1.0 / GROUPS) + se[rows]
            work[rows] = value
            return total + value * value

        total = lax.fori_loop(0, SIDE // STEP, add, jnp.zeros((STEP, SIDE), jnp.float32), unroll=True)
        scale, wide = scale_of(total)
        inverse = 1.0 / (LINEAR_SPAN * wide)

        def code(n, carry):
            rows = pl.ds(pl.multiple_of(n * STEP, STEP), STEP)
            value = work[rows]
            level = jnp.clip(value * inverse, -1.0, 1.0).astype(jnp.bfloat16)
            decoded = wide * level.astype(jnp.float32)
            nm[grp, rows] = decoded.astype(jnp.bfloat16)
            nse[rows] = value - decoded
            return carry

        lax.fori_loop(0, SIDE // STEP, code, 0, unroll=True)
        block = nm.at[grp]
        remote(block, block, s_nm.at[grp], device(x, y_up, z, j))
        remote(block, block, s_nm.at[grp], device(x, y_down, z, j))
        remote(block, block, s_nm.at[grp], sibling)
        local(block, nm_out.at[grp], s_out.at[1])
        local(nse, nse_out, s_out.at[2])

    def spread_near():
        top, bottom = pl.ds(0, HALF), pl.ds(HALF, HALF)
        for yy, target, rows, which in ((y_down, y_up, top, 0), (y_up, y_down, bottom, 1)):
            at = 2 * yy + j
            wait(nm.at[at], s_nm.at[at])
            remote(nm.at[at, rows], nm.at[at, rows], s_half.at[which], device(x, target, z, j))
            remote(nm.at[at], nm.at[at], s_nm.at[at], sibling)
            local(nm.at[at], nm_out.at[at], s_out.at[1])

    def spread_far():
        at = 2 * lax.rem(y + 2, NY) + j
        wait(nm.at[at, pl.ds(0, HALF)], s_half.at[0])
        wait(nm.at[at, pl.ds(HALF, HALF)], s_half.at[1])
        remote(nm.at[at], nm.at[at], s_nm.at[at], sibling)
        local(nm.at[at], nm_out.at[at], s_out.at[1])

    def take(core):
        for hop in (0, 1, 3, 2):
            at = 2 * lax.rem(y + hop, NY) + core
            wait(nm.at[at], s_nm.at[at])
            local(nm.at[at], nm_out.at[at], s_out.at[1])

    def drain_levels(c, carry):
        @pl.when(stretch_of(y, j, c) != grp)
        def _():
            wait(lev.at[c], s_send)

        return carry

    def drain(i, carry):
        wait(tok_a.at[i], s_send)
        wait(tok_b.at[i, 0], s_send)
        wait(tok_b.at[i, 1, pl.ds(0, 6)], s_send)
        wait(sent_far.at[i], s_send)

        @pl.when(jnp.logical_not(home))
        def _():
            wait(sent_own.at[i], s_send)
            wait(tok_a.at[i, 0], s_send)

        @pl.when(home)
        def _():
            wait(tok_a.at[i, 0, 0], s_send)

        return carry

    def drain_gather():
        lax.fori_loop(0, PIECES, drain, 0)
        wait(up_ref, s_send)
        wait(up_a.at[1, :, 0], s_send)
        wait(up_b.at[1, 0], s_send)
        lax.fori_loop(0, GROUPS, drain_levels, 0)

    def stage(s, i, carry):
        if s == 0:
            block = tok_a.at[i, z, q]
            wait(block, s_dist.at[i, 0])
            remote(block, block, s_ax.at[i], inner)
            block = tok_b.at[i, q, z]
            wait(block, s_dist.at[i, 1])
            remote(block, block, s_bz.at[i, 0, 0], above)
            remote(block, block, s_bz.at[i, 0, 1], below)
            remote(block, block, s_bx.at[i], inner)
        else:
            if s == 1:
                wait(tok_a.at[i, z, 1 - q], s_ax.at[i])
                block = tok_a.at[i, z]
                remote(block, block, s_az.at[i, 0, 0], above)
                remote(block, block, s_az.at[i, 0, 1], below)
            elif s <= 3:
                for way, sign, target in ((0, -1, above), (1, 1, below)):
                    block = tok_a.at[i, z_at(sign * (s - 1))]
                    wait(block, s_az.at[i, s - 2, way])
                    remote(block, block, s_az.at[i, s - 1, way], target)
            elif s == 4:
                for way, sign, target in ((0, -1, above), (1, 1, below)):
                    block = tok_a.at[i, z_at(sign * 3)]
                    wait(block, s_az.at[i, 2, way])
                    part = tok_a.at[i, z_at(sign * 3), way]
                    remote(part, part, s_az.at[i, 3, way], target)
            else:
                for way in range(2):
                    wait(tok_a.at[i, z_at(4), way], s_az.at[i, 3, way])
            if s <= 2:
                for way, sign, target in ((0, -1, above), (1, 1, below)):
                    block = tok_b.at[i, q, z_at(sign * s)]
                    wait(block, s_bz.at[i, s - 1, way])
                    remote(block, block, s_bz.at[i, s, way], target)
                    remote(block, block, s_bx.at[i], inner)
            elif s == 3:
                for way, sign, target in ((0, -1, above), (1, 1, below)):
                    block = tok_b.at[i, q, z_at(sign * 3)]
                    wait(block, s_bz.at[i, 2, way])
                    part = tok_b.at[i, q, z_at(sign * 3), pl.ds(32 * way, 32)]
                    remote(part, part, s_bz.at[i, 3, way], target)
                    remote(block, block, s_bx.at[i], inner)
            elif s == 4:
                for way in range(2):
                    wait(tok_b.at[i, q, z_at(4), pl.ds(32 * way, 32)], s_bz.at[i, 3, way])
                block = tok_b.at[i, q, z_at(4)]
                remote(block, block, s_bx.at[i], inner)
            else:
                wait(tok_b.at[i, 1 - q], s_bx.at[i])
        return carry

    def tick(t, carry):
        for s in range(6):
            lax.fori_loop(entered(t - s - 1), entered(t - s), functools.partial(stage, s), 0)

        @pl.when(home & (t == UP_AT))
        def _():
            for k in range(2):
                local(up_ref.at[k], up_a.at[0, :, k], s_up.at[k])
                local(up_ref.at[3 - k], up_b.at[0, k], s_up.at[2 + k])
            for k in range(2):
                remote(up_ref.at[k], up_a.at[0, :, k], s_up.at[k], sibling)
                remote(up_ref.at[3 - k], up_b.at[0, k], s_up.at[2 + k], sibling)

        @pl.when(t == LOAD_AT)
        def _():
            local(mom_ref, mom, s_in.at[0])
            local(we_ref, we, s_in.at[1])
            local(se_ref, se, s_in.at[2])

        @pl.when(t == RELAY)
        def _():
            block = up_a.at[1, :, j]
            wait(block, s_far.at[0])
            remote(block, block, s_relay.at[0], sibling)
            block = up_b.at[1, j]
            wait(block, s_far.at[1])
            remote(block, block, s_relay.at[1], sibling)

        @pl.when(t == FIRST_MM)
        def _():
            for k in range(2):
                wait(up_a.at[0, :, k], s_up.at[k])
                wait(up_b.at[0, k], s_up.at[2 + k])
            wait(up_a.at[1, :, 1 - j], s_relay.at[0])
            wait(up_b.at[1, 1 - j], s_relay.at[1])
            wait(mom, s_in.at[0])
            wait(we, s_in.at[1])
            wait(se, s_in.at[2])

        lax.fori_loop(done_pieces(t - 1), done_pieces(t), matmul, 0)
        lax.fori_loop(done_stretches(t - 1), done_stretches(t), compress, 0)

        pl.when(t == jnp.where(j == 0, OWN[0], OWN[1]))(own)
        pl.when(t == DRAIN)(drain_gather)
        pl.when(t == jnp.where(j == 0, NEAR[0], NEAR[1]))(spread_near)
        pl.when(t == jnp.where(j == 0, FAR[0], FAR[1]))(spread_far)

        @pl.when(t == jnp.where(j == 0, TAKE[1], TAKE[0]))
        def _():
            take(1 - j)

        return carry

    lax.fori_loop(0, TICKS, tick, 0)

    for _ in range(7):
        wait(nm.at[0], s_send)
    wait(nwe, s_out.at[0])
    wait(nm, s_out.at[1])
    wait(nse, s_out.at[2])


def tidy(nm_ref, nwe_ref, nse_ref, nm_out, nwe_out, nse_out, sems):
    pairs = ((nwe_ref, nwe_out), (nm_ref, nm_out), (nse_ref, nse_out))
    copies = [pltpu.make_async_copy(src, dst, sems.at[n]) for n, (src, dst) in enumerate(pairs)]
    for copy in copies:
        copy.start()
    for copy in copies:
        copy.wait()


def body(tokens, upstream, momentum, worker_error, server_error):
    bf16, f32 = jnp.bfloat16, jnp.float32
    anywhere = pl.BlockSpec(memory_space=pl.ANY)
    dma = pltpu.SemaphoreType.DMA
    stretches = (GROUPS, SIDE, SIDE)
    new_momentum, new_worker_error, new_server_error = pl.pallas_call(
        kernel,
        out_shape=(
            pltpu.VMEM(stretches, bf16),
            pltpu.VMEM(stretches, bf16),
            pltpu.VMEM((SIDE, SIDE), f32),
        ),
        in_specs=[anywhere] * 5,
        out_specs=[anywhere] * 3,
        scratch_shapes=[
            pltpu.VMEM((PIECES, NZ, 2, ROWS, PIECE), bf16),
            pltpu.VMEM((PIECES, 2, NZ, ROWS, PIECE), bf16),
            pltpu.VMEM((2, NZ, 2, ROWS, SIDE), bf16),
            pltpu.VMEM((2, 2, NZ, ROWS, SIDE), bf16),
            pltpu.VMEM((2 * PIECES, PIECE, SIDE), bf16),
            pltpu.VMEM((PIECES, PIECE, SIDE), bf16),
            pltpu.VMEM((PIECES, PIECE, SIDE), bf16),
            pltpu.VMEM(stretches, bf16),
            pltpu.VMEM(stretches, bf16),
            pltpu.VMEM(stretches, bf16),
            pltpu.VMEM((GROUPS, SIDE + HEAD, SIDE), bf16),
            pltpu.VMEM((GROUPS, SIDE + HEAD, SIDE), bf16),
            pltpu.VMEM(stretches, bf16),
            pltpu.VMEM((SIDE, SIDE), f32),
            pltpu.VMEM((SIDE, SIDE), f32),
            pltpu.VMEM((SIDE, SIDE), f32),
            dma((3,)),
            dma,
            dma((PIECES, 2)),
            dma((PIECES,)),
            dma((PIECES, 4, 2)),
            dma((PIECES,)),
            dma((PIECES, 4, 2)),
            dma((4,)),
            dma((2,)),
            dma((2,)),
            dma((2 * PIECES,)),
            dma((GROUPS,)),
            dma((GROUPS,)),
            dma((2,)),
            dma((3,)),
        ],
        name="compressed_step",
        compiler_params=pltpu.CompilerParams(
            collective_id=0, has_side_effects=True, vmem_limit_bytes=36 * 1024 * 1024
        ),
    )(
        *[
            pltpu.with_memory_space_constraint(value, pltpu.HBM)
            for value in (
                tokens[0],
                upstream[0].reshape(NX, NZ, ROWS, SIDE),
                momentum.reshape(stretches),
                worker_error[0].reshape(stretches),
                server_error,
            )
        ]
    )
    new_momentum, new_worker_error, new_server_error = pl.pallas_call(
        tidy,
        out_shape=(
            jax.ShapeDtypeStruct(stretches, bf16),
            jax.ShapeDtypeStruct(stretches, bf16),
            jax.ShapeDtypeStruct((SIDE, SIDE), f32),
        ),
        in_specs=[anywhere] * 3,
        out_specs=[anywhere] * 3,
        scratch_shapes=[dma((3,))],
        name="tidy",
        compiler_params=pltpu.CompilerParams(vmem_limit_bytes=1024 * 1024),
    )(*[pltpu.with_memory_space_constraint(value, pltpu.VMEM) for value in (new_momentum, new_worker_error, new_server_error)])
    return (
        new_momentum.reshape(GROUPS * SIDE, SIDE),
        new_worker_error.reshape(1, GROUPS * SIDE, SIDE),
        new_server_error,
    )


def solution(mesh):
    placed = (
        P("grp", "rep", None),
        P("grp", None, "rep"),
        P(None, "rep"),
        P("grp", None, "rep"),
        P("grp", "rep"),
    )
    return jax.shard_map(
        body,
        mesh=mesh,
        in_specs=placed,
        out_specs=(P(None, "rep"), P("grp", None, "rep"), P("grp", "rep")),
        check_vma=False,
    )
```

```python
import functools

import jax
import jax.numpy as jnp
from jax import lax
from jax.experimental import pallas as pl
from jax.experimental.pallas import tpu as pltpu
from jax.sharding import PartitionSpec as P

DECAY_RATE = 0.9
LINEAR_SPAN = 0.0625
EPSILON = 1e-06
MESH = pl.DeviceIdType.MESH

NX, NY, NZ = 4, 4, 8
GROUPS = 8
ROWS = 64
SIDE = 384
PIECE = 128
PIECES = 12
HEAD = 16
STEP = 32
HALF = SIDE // 2

AHEAD = 1
FIRST_MM = 6
RELAY = 5
LAG = 2
LATE = 20
OWN = (16, 17)
NEAR = (17, 18)
FAR = (18, 19)
TAKE = (19, 20)
TICKS = 21
DRAIN = 17
UP_AT = 3
LOAD_AT = 5
EARLY = 7


def entered(tick):
    return jnp.where(tick < 0, 0, jnp.minimum(tick + 1 + AHEAD, PIECES))


def done_pieces(tick):
    return jnp.maximum(0, jnp.minimum(2 * (tick - FIRST_MM + 1), entered(tick - 5)))


def done_stretches(tick):
    return (2 * done_pieces(tick - jnp.where(tick < LATE, LAG, 1))) // 3


def stretch_of(y, core, c):
    pair = c // 2
    hop = jnp.where(pair == 0, 2, jnp.where(pair == 3, 0, jnp.where((pair == 1) == (core == 0), 1, 3)))
    return 2 * lax.rem(y + hop, NY) + lax.rem(c, 2)


def kernel(
    tok_ref, up_ref, mom_ref, we_ref, se_ref,
    nm_out, nwe_out, nse_out,
    tok_a, tok_b, up_a, up_b, grads, sent_own, sent_far, mom, we, nwe, lev, got, nm, se, work, nse,
    s_in, s_send, s_dist, s_ax, s_az, s_bx, s_bz, s_up, s_far, s_relay, s_grad, s_lev, s_nm, s_half, s_out,
):
    grp = lax.axis_index("grp")
    rep = lax.axis_index("rep")
    y, j = grp // 2, lax.rem(grp, 2)
    x, z = rep // NZ, lax.rem(rep, NZ)
    h = x // 2
    q = lax.rem((x + 1) // 2, 2)
    x_in = x + 1 - 2 * lax.rem(x, 2)
    x_far = 3 - x
    z_up, z_down = lax.rem(z + 1, NZ), lax.rem(z + NZ - 1, NZ)
    y_up, y_down = lax.rem(y + 1, NY), lax.rem(y + NY - 1, NY)
    home = j == h

    def device(xx, yy, zz, core):
        return (2 * yy + core, NZ * xx + zz)

    inner = device(x_in, y, z, j)
    above = device(x, y, z_up, j)
    below = device(x, y, z_down, j)
    sibling = device(x, y, z, 1 - j)

    def remote(src, dst, sem, target):
        pltpu.make_async_remote_copy(
            src_ref=src, dst_ref=dst, send_sem=s_send, recv_sem=sem, device_id=target, device_id_type=MESH
        ).start()

    def local(src, dst, sem):
        pltpu.make_async_copy(src, dst, sem).start()

    def wait(ref, sem):
        pltpu.make_async_copy(ref, ref, sem).wait()

    barrier = pltpu.get_barrier_semaphore()
    greeted = [inner, above, below, device(x_far, y, z, 0), device(x_far, y, z, 1), sibling]
    for hop in range(1, NY):
        for core in range(2):
            greeted.append(device(x, lax.rem(y + hop, NY), z, core))
    for target in greeted:
        pl.semaphore_signal(barrier, inc=1, device_id=target, device_id_type=MESH)
    pl.semaphore_wait(barrier, len(greeted))

    near_x = jnp.where(home, x, x_far)

    def distribute(i, carry):
        for core in range(2):
            piece = 2 * i + core
            column = stretch_of(y, j, piece // 3) * SIDE + lax.rem(piece, 3) * PIECE
            src = tok_ref.at[:, pl.ds(pl.multiple_of(column, PIECE), PIECE)]
            for half in range(2):
                dst = tok_a.at[i, z, q] if half == 0 else tok_b.at[i, q, z]
                sem = s_dist.at[i, half]
                if core == half:

                    @pl.when((h == half) & home)
                    def _():
                        local(src, dst, sem)

                    @pl.when((h == half) & jnp.logical_not(home))
                    def _():
                        remote(src, dst, sem, device(x_far, y, z, core))
                else:

                    @pl.when(h == half)
                    def _():
                        remote(src, dst, sem, device(near_x, y, z, core))

        return carry

    lax.fori_loop(0, EARLY, distribute, 0)

    @pl.when(jnp.logical_not(home))
    def _():
        for k in range(2):
            remote(up_ref.at[k], up_a.at[1, :, k], s_far.at[0], device(x_far, y, z, k))
            remote(up_ref.at[3 - k], up_b.at[1, k], s_far.at[1], device(x_far, y, z, k))

    lax.fori_loop(EARLY, PIECES, distribute, 0)

    z_at = lambda d: lax.rem(z + d + NZ, NZ)

    def matmul(i, carry):
        left_a = tok_a[i].reshape(16 * ROWS, PIECE)
        left_b = tok_b[i].reshape(16 * ROWS, PIECE)
        contract = (((0,), (0,)), ((), ()))
        piece = 2 * i + j

        def product(slot):
            one = lax.dot_general(left_a, up_a[slot].reshape(16 * ROWS, SIDE), contract, preferred_element_type=jnp.float32)
            two = lax.dot_general(left_b, up_b[slot].reshape(16 * ROWS, SIDE), contract, preferred_element_type=jnp.float32)
            return (one + two).astype(jnp.bfloat16)

        sent_far[i] = product(1)
        remote(sent_far.at[i], grads.at[piece], s_grad.at[piece], device(x_far, y, z, h))
        own = product(0)

        @pl.when(home)
        def _():
            grads[piece] = own

        @pl.when(jnp.logical_not(home))
        def _():
            sent_own[i] = own
            remote(sent_own.at[i], grads.at[piece], s_grad.at[piece], sibling)

        return carry

    def scale_of(total):
        energy = jnp.sum(jnp.sum(total, axis=0, keepdims=True), axis=1, keepdims=True) * (1.0 / (SIDE * SIDE))
        scale = jnp.sqrt(energy + EPSILON).astype(jnp.bfloat16)
        return scale, scale.astype(jnp.float32)

    def compress(c, carry):
        at = stretch_of(y, j, c)
        total = jnp.zeros((STEP, SIDE), jnp.float32)
        for m in range(3):
            piece = 3 * c + m

            @pl.when(jnp.logical_not(home & (lax.rem(piece, 2) == j)))
            def _():
                wait(grads.at[piece], s_grad.at[piece])

            def add(n, total, m=m, piece=piece):
                row = n * STEP
                rows = pl.ds(pl.multiple_of(m * PIECE + row, STEP), STEP)
                value = (
                    DECAY_RATE * mom[at, rows].astype(jnp.float32)
                    + (1.0 - DECAY_RATE) * grads[piece, pl.ds(pl.multiple_of(row, STEP), STEP)].astype(jnp.float32)
                    + we[at, rows].astype(jnp.float32)
                )
                work[rows] = value
                return total + value * value

            total = lax.fori_loop(0, PIECE // STEP, add, total, unroll=True)
        scale, wide = scale_of(total)
        inverse = 1.0 / (LINEAR_SPAN * wide)
        lev[c, pl.ds(SIDE, HEAD)] = jnp.broadcast_to(scale, (HEAD, SIDE))

        def code(n, carry):
            rows = pl.ds(pl.multiple_of(n * STEP, STEP), STEP)
            value = work[rows]
            level = jnp.clip(value * inverse, -1.0, 1.0).astype(jnp.bfloat16)
            lev[c, rows] = level
            nwe[c, rows] = (value - wide * level.astype(jnp.float32)).astype(jnp.bfloat16)
            return carry

        lax.fori_loop(0, SIDE // STEP, code, 0, unroll=True)
        mine = at == grp

        @pl.when(mine)
        def _():
            local(lev.at[c], got.at[grp], s_lev.at[grp])

        @pl.when(jnp.logical_not(mine))
        def _():
            remote(lev.at[c], got.at[grp], s_lev.at[grp], (at, rep))

        local(nwe.at[c], nwe_out.at[at], s_out.at[0])
        return carry

    def own():
        for k in range(GROUPS):
            wait(got.at[k], s_lev.at[k])
        scales = [got[k, pl.ds(SIDE, HEAD)][0:1].astype(jnp.float32) for k in range(GROUPS)]

        def add(n, total):
            rows = pl.ds(pl.multiple_of(n * STEP, STEP), STEP)
            value = scales[0] * got[0, rows].astype(jnp.float32)
            for k in range(1, GROUPS):
                value += scales[k] * got[k, rows].astype(jnp.float32)
            value = value * (1.0 / GROUPS) + se[rows]
            work[rows] = value
            return total + value * value

        total = lax.fori_loop(0, SIDE // STEP, add, jnp.zeros((STEP, SIDE), jnp.float32), unroll=True)
        scale, wide = scale_of(total)
        inverse = 1.0 / (LINEAR_SPAN * wide)

        def code(n, carry):
            rows = pl.ds(pl.multiple_of(n * STEP, STEP), STEP)
            value = work[rows]
            level = jnp.clip(value * inverse, -1.0, 1.0).astype(jnp.bfloat16)
            decoded = wide * level.astype(jnp.float32)
            nm[grp, rows] = decoded.astype(jnp.bfloat16)
            nse[rows] = value - decoded
            return carry

        lax.fori_loop(0, SIDE // STEP, code, 0, unroll=True)
        block = nm.at[grp]
        remote(block, block, s_nm.at[grp], device(x, y_up, z, j))
        remote(block, block, s_nm.at[grp], device(x, y_down, z, j))
        remote(block, block, s_nm.at[grp], sibling)
        local(block, nm_out.at[grp], s_out.at[1])
        local(nse, nse_out, s_out.at[2])

    def spread_near():
        top, bottom = pl.ds(0, HALF), pl.ds(HALF, HALF)
        for yy, target, rows, which in ((y_down, y_up, top, 0), (y_up, y_down, bottom, 1)):
            at = 2 * yy + j
            wait(nm.at[at], s_nm.at[at])
            remote(nm.at[at, rows], nm.at[at, rows], s_half.at[which], device(x, target, z, j))
            remote(nm.at[at], nm.at[at], s_nm.at[at], sibling)
            local(nm.at[at], nm_out.at[at], s_out.at[1])

    def spread_far():
        at = 2 * lax.rem(y + 2, NY) + j
        wait(nm.at[at, pl.ds(0, HALF)], s_half.at[0])
        wait(nm.at[at, pl.ds(HALF, HALF)], s_half.at[1])
        remote(nm.at[at], nm.at[at], s_nm.at[at], sibling)
        local(nm.at[at], nm_out.at[at], s_out.at[1])

    def take(core):
        for hop in (0, 1, 3, 2):
            at = 2 * lax.rem(y + hop, NY) + core
            wait(nm.at[at], s_nm.at[at])
            local(nm.at[at], nm_out.at[at], s_out.at[1])

    def drain_levels(c, carry):
        @pl.when(stretch_of(y, j, c) != grp)
        def _():
            wait(lev.at[c], s_send)

        return carry

    def drain(i, carry):
        wait(tok_a.at[i], s_send)
        wait(tok_b.at[i, 0], s_send)
        wait(tok_b.at[i, 1, pl.ds(0, 6)], s_send)
        wait(sent_far.at[i], s_send)

        @pl.when(jnp.logical_not(home))
        def _():
            wait(sent_own.at[i], s_send)
            wait(tok_a.at[i, 0], s_send)

        @pl.when(home)
        def _():
            wait(tok_a.at[i, 0, 0], s_send)

        return carry

    def drain_gather():
        lax.fori_loop(0, PIECES, drain, 0)
        wait(up_ref, s_send)
        wait(up_a.at[1, :, 0], s_send)
        wait(up_b.at[1, 0], s_send)
        lax.fori_loop(0, GROUPS, drain_levels, 0)

    def stage(s, i, carry):
        if s == 0:
            block = tok_a.at[i, z, q]
            wait(block, s_dist.at[i, 0])
            remote(block, block, s_ax.at[i], inner)
            block = tok_b.at[i, q, z]
            wait(block, s_dist.at[i, 1])
            remote(block, block, s_bz.at[i, 0, 0], above)
            remote(block, block, s_bz.at[i, 0, 1], below)
            remote(block, block, s_bx.at[i], inner)
        else:
            if s == 1:
                wait(tok_a.at[i, z, 1 - q], s_ax.at[i])
                block = tok_a.at[i, z]
                remote(block, block, s_az.at[i, 0, 0], above)
                remote(block, block, s_az.at[i, 0, 1], below)
            elif s <= 3:
                for way, sign, target in ((0, -1, above), (1, 1, below)):
                    block = tok_a.at[i, z_at(sign * (s - 1))]
                    wait(block, s_az.at[i, s - 2, way])
                    remote(block, block, s_az.at[i, s - 1, way], target)
            elif s == 4:
                for way, sign, target in ((0, -1, above), (1, 1, below)):
                    block = tok_a.at[i, z_at(sign * 3)]
                    wait(block, s_az.at[i, 2, way])
                    part = tok_a.at[i, z_at(sign * 3), way]
                    remote(part, part, s_az.at[i, 3, way], target)
            else:
                for way in range(2):
                    wait(tok_a.at[i, z_at(4), way], s_az.at[i, 3, way])
            if s <= 2:
                for way, sign, target in ((0, -1, above), (1, 1, below)):
                    block = tok_b.at[i, q, z_at(sign * s)]
                    wait(block, s_bz.at[i, s - 1, way])
                    remote(block, block, s_bz.at[i, s, way], target)
                    remote(block, block, s_bx.at[i], inner)
            elif s == 3:
                for way, sign, target in ((0, -1, above), (1, 1, below)):
                    block = tok_b.at[i, q, z_at(sign * 3)]
                    wait(block, s_bz.at[i, 2, way])
                    part = tok_b.at[i, q, z_at(sign * 3), pl.ds(32 * way, 32)]
                    remote(part, part, s_bz.at[i, 3, way], target)
                    remote(block, block, s_bx.at[i], inner)
            elif s == 4:
                for way in range(2):
                    wait(tok_b.at[i, q, z_at(4), pl.ds(32 * way, 32)], s_bz.at[i, 3, way])
                block = tok_b.at[i, q, z_at(4)]
                remote(block, block, s_bx.at[i], inner)
            else:
                wait(tok_b.at[i, 1 - q], s_bx.at[i])
        return carry

    def tick(t, carry):
        for s in range(6):
            lax.fori_loop(entered(t - s - 1), entered(t - s), functools.partial(stage, s), 0)

        @pl.when(home & (t == UP_AT))
        def _():
            for k in range(2):
                local(up_ref.at[k], up_a.at[0, :, k], s_up.at[k])
                local(up_ref.at[3 - k], up_b.at[0, k], s_up.at[2 + k])
            for k in range(2):
                remote(up_ref.at[k], up_a.at[0, :, k], s_up.at[k], sibling)
                remote(up_ref.at[3 - k], up_b.at[0, k], s_up.at[2 + k], sibling)

        @pl.when(t == LOAD_AT)
        def _():
            local(mom_ref, mom, s_in.at[0])
            local(we_ref, we, s_in.at[1])
            local(se_ref, se, s_in.at[2])

        @pl.when(t == RELAY)
        def _():
            block = up_a.at[1, :, j]
            wait(block, s_far.at[0])
            remote(block, block, s_relay.at[0], sibling)
            block = up_b.at[1, j]
            wait(block, s_far.at[1])
            remote(block, block, s_relay.at[1], sibling)

        @pl.when(t == FIRST_MM)
        def _():
            for k in range(2):
                wait(up_a.at[0, :, k], s_up.at[k])
                wait(up_b.at[0, k], s_up.at[2 + k])
            wait(up_a.at[1, :, 1 - j], s_relay.at[0])
            wait(up_b.at[1, 1 - j], s_relay.at[1])
            wait(mom, s_in.at[0])
            wait(we, s_in.at[1])
            wait(se, s_in.at[2])

        lax.fori_loop(done_pieces(t - 1), done_pieces(t), matmul, 0)
        lax.fori_loop(done_stretches(t - 1), done_stretches(t), compress, 0)

        pl.when(t == jnp.where(j == 0, OWN[0], OWN[1]))(own)
        pl.when(t == DRAIN)(drain_gather)
        pl.when(t == jnp.where(j == 0, NEAR[0], NEAR[1]))(spread_near)
        pl.when(t == jnp.where(j == 0, FAR[0], FAR[1]))(spread_far)

        @pl.when(t == jnp.where(j == 0, TAKE[1], TAKE[0]))
        def _():
            take(1 - j)

        return carry

    lax.fori_loop(0, TICKS, tick, 0)

    for _ in range(7):
        wait(nm.at[0], s_send)
    wait(nwe, s_out.at[0])
    wait(nm, s_out.at[1])
    wait(nse, s_out.at[2])


def tidy(nm_ref, nwe_ref, nse_ref, nm_out, nwe_out, nse_out, sems):
    pairs = ((nwe_ref, nwe_out), (nm_ref, nm_out), (nse_ref, nse_out))
    copies = [pltpu.make_async_copy(src, dst, sems.at[n]) for n, (src, dst) in enumerate(pairs)]
    for copy in copies:
        copy.start()
    for copy in copies:
        copy.wait()


def body(tokens, upstream, momentum, worker_error, server_error):
    bf16, f32 = jnp.bfloat16, jnp.float32
    anywhere = pl.BlockSpec(memory_space=pl.ANY)
    dma = pltpu.SemaphoreType.DMA
    stretches = (GROUPS, SIDE, SIDE)
    new_momentum, new_worker_error, new_server_error = pl.pallas_call(
        kernel,
        out_shape=(
            pltpu.VMEM(stretches, bf16),
            pltpu.VMEM(stretches, bf16),
            pltpu.VMEM((SIDE, SIDE), f32),
        ),
        in_specs=[anywhere] * 5,
        out_specs=[anywhere] * 3,
        scratch_shapes=[
            pltpu.VMEM((PIECES, NZ, 2, ROWS, PIECE), bf16),
            pltpu.VMEM((PIECES, 2, NZ, ROWS, PIECE), bf16),
            pltpu.VMEM((2, NZ, 2, ROWS, SIDE), bf16),
            pltpu.VMEM((2, 2, NZ, ROWS, SIDE), bf16),
            pltpu.VMEM((2 * PIECES, PIECE, SIDE), bf16),
            pltpu.VMEM((PIECES, PIECE, SIDE), bf16),
            pltpu.VMEM((PIECES, PIECE, SIDE), bf16),
            pltpu.VMEM(stretches, bf16),
            pltpu.VMEM(stretches, bf16),
            pltpu.VMEM(stretches, bf16),
            pltpu.VMEM((GROUPS, SIDE + HEAD, SIDE), bf16),
            pltpu.VMEM((GROUPS, SIDE + HEAD, SIDE), bf16),
            pltpu.VMEM(stretches, bf16),
            pltpu.VMEM((SIDE, SIDE), f32),
            pltpu.VMEM((SIDE, SIDE), f32),
            pltpu.VMEM((SIDE, SIDE), f32),
            dma((3,)),
            dma,
            dma((PIECES, 2)),
            dma((PIECES,)),
            dma((PIECES, 4, 2)),
            dma((PIECES,)),
            dma((PIECES, 4, 2)),
            dma((4,)),
            dma((2,)),
            dma((2,)),
            dma((2 * PIECES,)),
            dma((GROUPS,)),
            dma((GROUPS,)),
            dma((2,)),
            dma((3,)),
        ],
        name="compressed_step",
        compiler_params=pltpu.CompilerParams(
            collective_id=0, has_side_effects=True, vmem_limit_bytes=36 * 1024 * 1024
        ),
    )(
        *[
            pltpu.with_memory_space_constraint(value, pltpu.HBM)
            for value in (
                tokens[0],
                upstream[0].reshape(NX, NZ, ROWS, SIDE),
                momentum.reshape(stretches),
                worker_error[0].reshape(stretches),
                server_error,
            )
        ]
    )
    new_momentum, new_worker_error, new_server_error = pl.pallas_call(
        tidy,
        out_shape=(
            jax.ShapeDtypeStruct(stretches, bf16),
            jax.ShapeDtypeStruct(stretches, bf16),
            jax.ShapeDtypeStruct((SIDE, SIDE), f32),
        ),
        in_specs=[anywhere] * 3,
        out_specs=[anywhere] * 3,
        scratch_shapes=[dma((3,))],
        name="tidy",
        compiler_params=pltpu.CompilerParams(vmem_limit_bytes=1024 * 1024),
    )(*[pltpu.with_memory_space_constraint(value, pltpu.VMEM) for value in (new_momentum, new_worker_error, new_server_error)])
    return (
        new_momentum.reshape(GROUPS * SIDE, SIDE),
        new_worker_error.reshape(1, GROUPS * SIDE, SIDE),
        new_server_error,
    )


def solution(mesh):
    placed = (
        P("grp", "rep", None),
        P("grp", None, "rep"),
        P(None, "rep"),
        P("grp", None, "rep"),
        P("grp", "rep"),
    )
    return jax.shard_map(
        body,
        mesh=mesh,
        in_specs=placed,
        out_specs=(P(None, "rep"), P("grp", None, "rep"), P("grp", "rep")),
        check_vma=False,
    )
```
